256 devices in a mesh: expert: 64 (over z, x, core), replica: 4 (over y).
Axes of the slice: x: 4, y: 4, z: 8, core: 2. Of those that a mesh axis runs over, the one named last changes fastest.
Arguments:
- tokens: bfloat16 [49152, 3584], P(('expert', 'replica')), may hold values from -6 to 6
- routes: int32 [49152], P(('expert', 'replica')), may hold values from 0 to 64, as said below
- combine_weights: float32 [49152], P(('expert', 'replica')), may hold values from 0.2 to 1
- up_weight: bfloat16 [64, 3584, 1024], P('expert', None, 'replica'), may hold values from -0.09375 to 0.09375
- down_weight: bfloat16 [64, 1024, 3584], P('expert', 'replica'), may hold values from -0.1875 to 0.1875
- cotangent: bfloat16 [49152, 3584], P(('expert', 'replica')), may hold values from -6 to 6
Outputs:
- mixed: bfloat16 [49152, 3584], P(('expert', 'replica'))
- token_grads: bfloat16 [49152, 3584], P(('expert', 'replica'))
- combine_grads: float32 [49152], P(('expert', 'replica'))
- up_grads: bfloat16 [64, 3584, 1024], P('expert', None, 'replica')
- down_grads: bfloat16 [64, 1024, 3584], P('expert', 'replica')
The draws below stay inside these ranges and needn't reach their ends.
Inputs may be any that keep to these rules, and one draw needn't show every extreme that they name: Among the 192 tokens of one device (aligned blocks of routes), no expert is named more than 3 times, and in every block some expert (not necessarily the same one in every block) is named exactly 3 times.
All inputs are finite; a program needn't handle non-finite values.
Results may differ from the reference program's by a relative error of at most 0.015.
Values may be sent and summed in bfloat16 or wider, within the bound.
A program may use at most 128 MiB of HBM per device.

```python
import jax
import jax.numpy as jnp
from jax import lax

D = 3584
FF = 1024
CAP = 3
EXPERTS = 64
TOK_DEV = 192
TOKENS = 49152
N_EXPERT = 64
N_REPLICA = 4


def draw_routes(key, part):
    key = jax.random.fold_in(key, 11)
    blocks = TOKENS // TOK_DEV
    hot_expert = jax.random.randint(jax.random.fold_in(key, 1), (), 0, EXPERTS).astype(jnp.int32)
    others = ((hot_expert + 1 + jnp.arange(EXPERTS - 1, dtype=jnp.int32)) % EXPERTS).astype(jnp.int32)
    draw_pool = jnp.concatenate([jnp.repeat(others, CAP), jnp.full((2 * TOK_DEV,), EXPERTS, jnp.int32)])

    def one_block(block_key):
        pick_key, order_key = jax.random.split(block_key)
        chosen = jax.random.permutation(pick_key, draw_pool)[:TOK_DEV - CAP]
        block_routes = jnp.concatenate([jnp.full((CAP,), hot_expert, jnp.int32), chosen])
        return jax.random.permutation(order_key, block_routes)
    block_keys = jax.random.split(jax.random.fold_in(key, 2), blocks)
    return jax.vmap(one_block)(block_keys).reshape(TOKENS).astype(jnp.int32)


def shard_levels(own_key, extent, cuts, smallest, high):
    factor_of = 1.0
    for dim, blocks in cuts:
        steps = jax.random.uniform(jax.random.fold_in(jax.random.fold_in(own_key, 6), dim), (blocks,), jnp.float32, smallest / len(cuts), high / len(cuts))
        factor_of = factor_of * jnp.repeat(jnp.exp(steps), extent[dim] // blocks).reshape((-1,) + (1,) * (len(extent) - 1 - dim))
    return factor_of


def gaussian(stream_key, extent, scale, bound, cuts=(), kind=jnp.bfloat16):
    entries = jax.random.normal(stream_key, extent, jnp.float32) * scale
    if len(cuts) > 0:
        entries = shard_levels(stream_key, extent, cuts, -0.22, 0.18) * entries
    return jnp.clip(entries, min=-bound, max=bound).astype(kind)


def setup_inputs(seed: int = 0) -> dict:
    streams_of = jax.random.split(jax.random.key(seed), 7)
    return {
        "tokens": gaussian(streams_of[0], (TOKENS, D), 1.0, 6.0, ((0, 256),)),
        "routes": draw_routes(jax.random.fold_in(streams_of[6], 71), 0),
        "combine_weights": jnp.clip(0.2 + 0.8 * jax.random.uniform(streams_of[2], (TOKENS,), jnp.float32) ** shard_levels(streams_of[2], (TOKENS,), ((0, 256),), -0.2, 0.2), 0.2, 1.0),
        "up_weight": gaussian(streams_of[3], (EXPERTS, D, FF), D ** -0.5, 0.09375, ((0, 64), (2, 4))),
        "down_weight": gaussian(streams_of[4], (EXPERTS, FF, D), FF ** -0.5, 0.1875, ((0, 64), (1, 4))),
        "cotangent": gaussian(streams_of[5], (TOKENS, D), 1.0, 6.0, ((0, 256),)),
    }


def silu_slope(pre_act):
    sigmoid_value = jax.nn.sigmoid(pre_act)
    return sigmoid_value * (1.0 + pre_act * (1.0 - sigmoid_value))


def reference(tokens, routes, combine_weights, up_weight, down_weight, cotangent):
    blocks = TOKENS // TOK_DEV
    experts = up_weight.shape[0]
    model_width = tokens.shape[1]
    block_width = FF // N_REPLICA
    block_routes = routes.reshape(blocks, TOK_DEV)
    labels = jnp.arange(experts, dtype=jnp.int32)
    onehot = (block_routes[:, :, None] == labels[None, None, :]).astype(jnp.int32)
    slot_rank = jnp.sum((jnp.cumsum(onehot, axis=1) - onehot) * onehot, axis=2)
    slot_of = jnp.where(block_routes < experts, block_routes * CAP + slot_rank, experts * CAP).astype(jnp.int32)
    position = jnp.arange(TOKENS, dtype=jnp.int32).reshape(blocks, TOK_DEV)
    block_index = jnp.broadcast_to(jnp.arange(blocks, dtype=jnp.int32)[:, None], (blocks, TOK_DEV))
    slot_owner = jnp.full((blocks, experts * CAP + 1), TOKENS, jnp.int32).at[block_index, slot_of].set(position)
    slot_owner = slot_owner[:, :experts * CAP].reshape(N_EXPERT, N_REPLICA, experts, CAP)
    slot_owner = jnp.transpose(slot_owner, (2, 1, 0, 3)).reshape(experts, N_REPLICA, N_EXPERT * CAP)

    def one_expert(inputs_of):
        slot_tokens, up_matrix, down_matrix = inputs_of
        filled = slot_tokens < TOKENS
        safe_index = jnp.where(filled, slot_tokens, 0)
        sent_rows = jnp.where(filled[..., None], tokens[safe_index], jnp.zeros((), tokens.dtype))
        scaled = combine_weights[safe_index][..., None] * cotangent[safe_index].astype(jnp.float32)
        out_grad = jnp.where(filled[..., None], scaled, jnp.zeros((), jnp.float32)).astype(jnp.bfloat16)
        up32 = up_matrix.astype(jnp.float32)
        down32 = down_matrix.astype(jnp.float32)
        pre_act = jnp.einsum("grd,df->grf", sent_rows.astype(jnp.float32), up32)
        hidden = jax.nn.silu(pre_act).astype(jnp.bfloat16)
        hidden_blocks = hidden.astype(jnp.float32).reshape(N_REPLICA, N_REPLICA, -1, N_REPLICA, block_width)
        down_blocks = down32.reshape(N_REPLICA, block_width, model_width)
        out_parts = jnp.einsum("grkf,kfd->kgrd", hidden_blocks.reshape(N_REPLICA, -1, N_REPLICA, block_width), down_blocks).astype(jnp.bfloat16)
        expert_out = jnp.sum(out_parts.astype(jnp.float32), axis=0).astype(jnp.bfloat16)
        hidden_grad = jnp.einsum("grd,fd->grf", out_grad.astype(jnp.float32), down32)
        pre_grad = (hidden_grad * silu_slope(pre_act)).astype(jnp.bfloat16)
        pre_blocks = pre_grad.astype(jnp.float32).reshape(N_REPLICA, -1, N_REPLICA, block_width)
        up_blocks = up32.reshape(model_width, N_REPLICA, block_width)
        row_parts = jnp.einsum("grkf,dkf->kgrd", pre_blocks, up_blocks).astype(jnp.bfloat16)
        row_grads = jnp.sum(row_parts.astype(jnp.float32), axis=0).astype(jnp.bfloat16)
        down_part = jnp.einsum("grf,grd->gfd", hidden.astype(jnp.float32), out_grad.astype(jnp.float32)).astype(jnp.bfloat16)
        up_part = jnp.einsum("grd,grf->gdf", sent_rows.astype(jnp.float32), pre_grad.astype(jnp.float32)).astype(jnp.bfloat16)
        down_grad = jnp.sum(down_part.astype(jnp.float32), axis=0).astype(jnp.bfloat16)
        up_grad = jnp.sum(up_part.astype(jnp.float32), axis=0).astype(jnp.bfloat16)
        return expert_out, row_grads, up_grad, down_grad

    expert_out, row_grads, up_grads, down_grads = lax.map(one_expert, (slot_owner, up_weight, down_weight))
    target = slot_owner.reshape(-1)
    token_out = jnp.zeros((TOKENS + 1, model_width), jnp.bfloat16).at[target].set(expert_out.reshape(-1, model_width))[:TOKENS]
    token_rows = jnp.zeros((TOKENS + 1, model_width), jnp.bfloat16).at[target].set(row_grads.reshape(-1, model_width))[:TOKENS]
    weights_col = combine_weights[:, None]
    mixed = (weights_col * token_out.astype(jnp.float32)).astype(jnp.bfloat16)
    combine_grads = jnp.sum(token_out.astype(jnp.float32) * cotangent.astype(jnp.float32), axis=1)
    token_grads = (weights_col * token_rows.astype(jnp.float32)).astype(jnp.bfloat16)
    return (mixed, token_grads, combine_grads, up_grads, down_grads)
```

```python
import functools
import math

import jax
import jax.numpy as jnp
import numpy as np
from jax import lax
from jax.experimental import pallas as pl
from jax.experimental.pallas import tpu as pltpu
from jax.sharding import PartitionSpec as P

CAP = 3
CHUNK = 512
MESH = pl.DeviceIdType.MESH
F32 = jnp.float32
BF16 = jnp.bfloat16
NN = (((1,), (0,)), ((), ()))
NT = (((1,), (1,)), ((), ()))
TN = (((0,), (0,)), ((), ()))


def mm(a, b, dims=NN):
    return lax.dot_general(a, b, dims, preferred_element_type=F32)


def wait_for(ref, sem):
    pltpu.make_async_copy(ref, ref, sem).wait()


def pack(rows, parts, half):
    m = rows.shape[0] // parts
    return [
        jnp.concatenate(
            [rows[p * m:(p + 1) * m, :half], rows[p * m:(p + 1) * m, half:]], axis=0
        ).astype(BF16)
        for p in range(parts)
    ]


def unpack(blocks, parts):
    m = blocks.shape[1] // 2
    wide = [blocks[p].astype(F32) for p in range(parts)]
    left = jnp.concatenate([b[:m] for b in wide], axis=0)
    right = jnp.concatenate([b[m:] for b in wide], axis=0)
    return jnp.concatenate([left, right], axis=1).astype(BF16)


def kernel(
    side, chunks,
    tok, cot, w_row, route_row, swap, wu, wd,
    mixed, token_grads, combine_grads, dwu, dwd,
    send_a, send_b, recv_a, recv_b, xg, wu_far, wd_far, acc, hid, pg,
    out_send, out_recv, dwu_send, dwd_send, dwu_recv, dwd_recv,
    pick, pick_t, w_col, cg, source,
    a_out, a_in, b_out, b_in, y_out, y_in, f_out, f_in, o_out, o_in, d_out, d_in,
):
    nt, width = tok.shape
    slots = side * side * CAP
    half = CHUNK // 2
    expert, y = lax.axis_index("expert"), lax.axis_index("replica")
    z, k = expert // side, expert % side
    row_pal = (expert, y + 1 - 2 * (y % 2))
    block_pal = (expert, 3 - y)
    steps = 2 * chunks

    barrier = pltpu.get_barrier_semaphore()
    for d in range(1, side):
        pl.semaphore_signal(barrier, inc=1, device_id=((z + d) % side * side + k, y), device_id_type=MESH)
        pl.semaphore_signal(barrier, inc=1, device_id=(z * side + (k + d) % side, y), device_id_type=MESH)
    pl.semaphore_signal(barrier, inc=1, device_id=row_pal, device_id_type=MESH)
    pl.semaphore_signal(barrier, inc=1, device_id=block_pal, device_id_type=MESH)

    down = lax.broadcasted_iota(jnp.int32, (nt, nt), 0)
    across = lax.broadcasted_iota(jnp.int32, (nt, nt), 1)
    eye = down == across
    routes = jnp.broadcast_to(route_row[...].astype(F32), (nt, nt))
    route_col = jnp.sum(jnp.where(eye, routes, 0.0), axis=1, keepdims=True)
    w_col[...] = jnp.sum(jnp.where(eye, jnp.broadcast_to(w_row[...], (nt, nt)), 0.0), axis=1, keepdims=True)
    same = routes == route_col
    rank_row = jnp.sum(jnp.where(same & (down < across), 1.0, 0.0), axis=0, keepdims=True)
    rank_col = jnp.sum(jnp.where(same & (across < down), 1.0, 0.0), axis=1, keepdims=True)
    limit = float(side * side)
    slot_row = jnp.where(routes[:1] < limit, routes[:1] * CAP + rank_row, float(slots))
    slot_col = jnp.where(route_col < limit, route_col * CAP + rank_col, float(slots))
    at_slot = lax.broadcasted_iota(jnp.int32, (slots, nt), 0).astype(F32)
    pick[...] = jnp.where(at_slot == slot_row, 1.0, 0.0).astype(BF16)
    at_slot = lax.broadcasted_iota(jnp.int32, (nt, slots), 1).astype(F32)
    pick_t[...] = jnp.where(at_slot == slot_col, 1.0, 0.0).astype(BF16)
    acc[...] = jnp.zeros_like(acc)
    cg[...] = jnp.zeros_like(cg)

    pl.semaphore_wait(barrier, 2 * side)

    def columns(j):
        return pl.ds(pl.multiple_of(j * CHUNK, CHUNK), CHUNK)

    order = sorted(range(1, side), key=lambda d: -min(d, side - d))

    def exchange_a(i, j):
        for d in order:
            to = (z + d) % side
            pltpu.make_async_remote_copy(
                send_a.at[j, to], recv_a.at[i, z], a_out.at[j], a_in.at[i],
                device_id=(to * side + k, y), device_id_type=MESH,
            ).start()
        pltpu.make_async_copy(send_a.at[j, z], recv_a.at[i, z], a_in.at[i]).start()

    def exchange_b(i, j):
        for d in order:
            to = (k + d) % side
            pltpu.make_async_remote_copy(
                send_b.at[j, to], recv_b.at[i, k], b_out.at[j], b_in.at[i],
                device_id=(z * side + to, y), device_id_type=MESH,
            ).start()
        pltpu.make_async_copy(send_b.at[j, k], recv_b.at[i, k], b_in.at[i]).start()

    def sent_a(j):
        wait_for(send_a.at[j, pl.ds(0, side - 1)], a_out.at[j])

    def sent_b(j):
        wait_for(send_b.at[j, pl.ds(0, side - 1)], b_out.at[j])

    def swapped(ref, i):
        blocks = ref[i]
        flat = blocks.reshape(blocks.shape[0] * blocks.shape[1], half)
        return mm(swap[...], flat).astype(BF16).reshape(blocks.shape)

    def far_weight(i, go):
        j = i % chunks

        @pl.when(i < chunks)
        def _():
            copy = pltpu.make_async_remote_copy(
                wu.at[columns(j), :], wu_far.at[j], f_out.at[i], f_in.at[i],
                device_id=block_pal, device_id_type=MESH)
            go(copy)

        @pl.when(i >= chunks)
        def _():
            copy = pltpu.make_async_remote_copy(
                wd.at[:, columns(j)], wd_far.at[j], f_out.at[i], f_in.at[i],
                device_id=block_pal, device_id_type=MESH)
            go(copy)

    def step_a(i):
        j = i % chunks

        @pl.when(i < chunks)
        def _():
            source[...] = tok[:, columns(j)]

        @pl.when(i >= chunks)
        def _():
            sent_a(j)
            source[...] = (w_col[...] * cot[:, columns(j)].astype(F32)).astype(BF16)

        for p, block in enumerate(pack(mm(pick[...], source[...]), side, half)):
            send_a[j, p] = block
        exchange_a(i, j)

    def step_b(i):
        j = i % chunks
        wait_for(recv_a.at[i], a_in.at[i])

        @pl.when(i >= chunks)
        def _():
            sent_b(j)

        send_b[j] = swapped(recv_a, i)
        exchange_b(i, j)

    def row_copy(i):
        return pltpu.make_async_remote_copy(
            xg.at[i, pl.ds(0, slots)], xg.at[i, pl.ds(slots, slots)], y_out.at[i], y_in.at[i],
            device_id=row_pal, device_id_type=MESH)

    def step_c(i):
        wait_for(recv_b.at[i], b_in.at[i])
        xg[i, pl.ds(0, slots)] = unpack(recv_b[i], side)
        row_copy(i).start()

    def step_d(i):
        j = i % chunks
        row_copy(i).wait_recv()
        far_weight(i, lambda copy: copy.wait_recv())

        @pl.when(i < chunks)
        def _():
            acc[0] += mm(xg[i], wu[columns(j), :])
            acc[1] += mm(xg[i], wu_far[j])

        @pl.when(i >= chunks)
        def _():
            acc[2] += mm(xg[i], wd[:, columns(j)], NT)
            acc[3] += mm(xg[i], wd_far[j], NT)

    def at(i, lag, step):
        @pl.when((i >= lag) & (i < steps + lag))
        def _():
            step(i - lag)

    AHEAD = 3
    for i in range(AHEAD):
        far_weight(jnp.int32(i), lambda copy: copy.start())

    LAG_D = 4

    def gather(i, _):
        at(i, 0, step_a)

        @pl.when(i + AHEAD < steps)
        def _():
            far_weight(i + AHEAD, lambda copy: copy.start())

        at(i, 1, step_b)
        at(i, 2, step_c)
        at(i, LAG_D, step_d)
        return 0

    lax.fori_loop(0, steps + LAG_D, gather, 0)

    for b in range(2):
        pre = acc[b]
        s = 1.0 / (1.0 + jnp.exp(-pre))
        hid[b] = (pre * s).astype(BF16)
        pg[b] = (acc[2 + b] * (s * (1.0 + pre * (1.0 - s)))).astype(BF16)


    def out_copy(i):
        j = i % chunks
        return pltpu.make_async_remote_copy(
            out_send.at[j], out_recv.at[i], o_out.at[j], o_in.at[i],
            device_id=row_pal, device_id_type=MESH)

    def dwd_copy(i):
        j = i % chunks
        return pltpu.make_async_remote_copy(
            dwd_send.at[j], dwd_recv.at[j], d_out.at[i], d_in.at[i],
            device_id=block_pal, device_id_type=MESH)

    def dwu_copy(i):
        j = i % chunks
        return pltpu.make_async_remote_copy(
            dwu_send.at[j], dwu_recv.at[j], d_out.at[i], d_in.at[i],
            device_id=block_pal, device_id_type=MESH)

    def out_rows(j, rows):
        return mm(hid[0, rows], wd[:, columns(j)]) + mm(hid[1, rows], wd_far[j])

    def grad_rows(j, rows):
        return mm(pg[0, rows], wu[columns(j), :], NT) + mm(pg[1, rows], wu_far[j], NT)

    near, far = pl.ds(0, slots), pl.ds(slots, slots)

    def step_e(i):
        j = i % chunks

        @pl.when(i < chunks)
        def _():
            out_send[j] = out_rows(j, far).astype(BF16)
            out_copy(i).start()
            dwd_send[j] = mm(hid[1], xg[chunks + j], TN).astype(BF16)
            dwd_copy(i).start()

        @pl.when(i >= chunks)
        def _():
            out_copy(i).wait_send()
            out_send[j] = grad_rows(j, far).astype(BF16)
            out_copy(i).start()
            dwu_send[j] = mm(xg[j], pg[1], TN).astype(BF16)
            dwu_copy(i).start()

    def step_f(i):
        j = i % chunks
        out_copy(i).wait_recv()
        sent_b(j)

        @pl.when(i < chunks)
        def _():
            for p, block in enumerate(pack(out_rows(j, near) + out_recv[i].astype(F32), side, half)):
                send_b[j, p] = block

        @pl.when(i >= chunks)
        def _():
            for p, block in enumerate(pack(grad_rows(j, near) + out_recv[i].astype(F32), side, half)):
                send_b[j, p] = block

        exchange_b(steps + i, j)

    def step_g(i):
        j = i % chunks
        wait_for(recv_b.at[steps + i], b_in.at[steps + i])
        sent_a(j)
        send_a[j] = swapped(recv_b, steps + i)
        exchange_a(steps + i, j)

    def step_h(i):
        j = i % chunks
        wait_for(recv_a.at[steps + i], a_in.at[steps + i])
        rows = mm(pick_t[...], unpack(recv_a[steps + i], side))
        scaled = (w_col[...] * rows).astype(BF16)

        @pl.when(i < chunks)
        def _():
            mixed[:, columns(j)] = scaled
            cg[...] += jnp.sum(rows * cot[:, columns(j)].astype(F32), axis=1, keepdims=True)

        @pl.when(i >= chunks)
        def _():
            token_grads[:, columns(j)] = scaled

    def step_i(i):
        j = i % chunks

        @pl.when(i < chunks)
        def _():
            dwd_copy(i).wait_recv()
            dwd[:, columns(j)] = (mm(hid[0], xg[chunks + j], TN) + dwd_recv[j].astype(F32)).astype(BF16)

        @pl.when(i >= chunks)
        def _():
            dwu_copy(i).wait_recv()
            dwu[columns(j), :] = (mm(xg[j], pg[0], TN) + dwu_recv[j].astype(F32)).astype(BF16)

    LAG_I = 4

    def scatter(i, _):
        at(i, 0, step_e)
        at(i, 1, step_f)
        at(i, 2, step_g)
        at(i, 3, step_h)
        at(i, LAG_I, step_i)
        return 0

    lax.fori_loop(0, steps + LAG_I, scatter, 0)

    combine_grads[...] = jnp.sum(jnp.where(eye, jnp.broadcast_to(cg[...], (nt, nt)), 0.0), axis=0, keepdims=True)

    def drain(j, _):
        sent_a(j)
        sent_b(j)
        out_copy(j + chunks).wait_send()
        dwd_copy(j).wait_send()
        dwu_copy(j + chunks).wait_send()
        return 0

    lax.fori_loop(0, chunks, drain, 0)

    def drain_all(i, _):
        row_copy(i).wait_send()
        far_weight(i, lambda copy: copy.wait_send())
        return 0

    lax.fori_loop(0, steps, drain_all, 0)


def swap_matrix(side):
    n = side * 2 * side * CAP
    index = np.arange(n).reshape(side, 2, side, CAP)
    source = index.transpose(2, 1, 0, 3).reshape(-1)
    matrix = np.zeros((n, n), np.float32)
    matrix[np.arange(n), source] = 1.0
    return matrix.astype(jnp.bfloat16)


def body(side, tokens, routes, combine_weights, up_weight, down_weight, cotangent):
    nt, width = tokens.shape
    block = up_weight.shape[2]
    chunks = width // CHUNK
    slots = side * side * CAP
    half = CHUNK // 2
    steps = 2 * chunks
    vmem = pl.BlockSpec(memory_space=pltpu.VMEM)
    message = (side, 2 * side * CAP, half)
    dma = pltpu.SemaphoreType.DMA
    mixed, token_grads, combine_grads, up_grads, down_grads = pl.pallas_call(
        functools.partial(kernel, side, chunks),
        out_shape=(
            jax.ShapeDtypeStruct((nt, width), BF16),
            jax.ShapeDtypeStruct((nt, width), BF16),
            jax.ShapeDtypeStruct((1, nt), F32),
            jax.ShapeDtypeStruct((width, block), BF16),
            jax.ShapeDtypeStruct((block, width), BF16),
        ),
        in_specs=[vmem] * 7,
        out_specs=(vmem,) * 5,
        scratch_shapes=[
            pltpu.VMEM((chunks,) + message, BF16),
            pltpu.VMEM((chunks,) + message, BF16),
            pltpu.VMEM((2 * steps,) + message, BF16),
            pltpu.VMEM((2 * steps,) + message, BF16),
            pltpu.VMEM((steps, 2 * slots, CHUNK), BF16),
            pltpu.VMEM((chunks, CHUNK, block), BF16),
            pltpu.VMEM((chunks, block, CHUNK), BF16),
            pltpu.VMEM((4, 2 * slots, block), F32),
            pltpu.VMEM((2, 2 * slots, block), BF16),
            pltpu.VMEM((2, 2 * slots, block), BF16),
            pltpu.VMEM((chunks, slots, CHUNK), BF16),
            pltpu.VMEM((steps, slots, CHUNK), BF16),
            pltpu.VMEM((chunks, CHUNK, block), BF16),
            pltpu.VMEM((chunks, block, CHUNK), BF16),
            pltpu.VMEM((chunks, CHUNK, block), BF16),
            pltpu.VMEM((chunks, block, CHUNK), BF16),
            pltpu.VMEM((slots, nt), BF16),
            pltpu.VMEM((nt, slots), BF16),
            pltpu.VMEM((nt, 1), F32),
            pltpu.VMEM((nt, 1), F32),
            pltpu.VMEM((nt, CHUNK), BF16),
            dma((chunks,)), dma((2 * steps,)),
            dma((chunks,)), dma((2 * steps,)),
            dma((steps,)), dma((steps,)),
            dma((steps,)), dma((steps,)),
            dma((chunks,)), dma((steps,)),
            dma((steps,)), dma((steps,)),
        ],
        compiler_params=pltpu.CompilerParams(
            collective_id=0, has_side_effects=True, vmem_limit_bytes=60 * 1024 * 1024
        ),
    )(
        tokens, cotangent, combine_weights[None], routes[None],
        jnp.asarray(swap_matrix(side)), up_weight[0], down_weight[0],
    )
    return mixed, token_grads, combine_grads[0], up_grads[None], down_grads[None]


def solution(mesh):
    side = math.isqrt(mesh.shape["expert"])
    row, vector = P(("expert", "replica"), None), P(("expert", "replica"))
    up, down = P("expert", None, "replica"), P("expert", "replica", None)
    return jax.shard_map(
        functools.partial(body, side),
        mesh=mesh,
        in_specs=(row, vector, vector, up, down, row),
        out_specs=(row, row, vector, up, down),
        check_vma=False,
    )
```

```python
import functools
import math

import jax
import jax.numpy as jnp
import numpy as np
from jax import lax
from jax.experimental import pallas as pl
from jax.experimental.pallas import tpu as pltpu
from jax.sharding import PartitionSpec as P

CAP = 3
CHUNK = 512
LAG_B, LAG_C, LAG_D = 1, 2, 4
LAG_F, LAG_G, LAG_H, LAG_W, LAG_I = 2, 3, 5, 4, 8
AHEAD = 6
MESH = pl.DeviceIdType.MESH
F32 = jnp.float32
BF16 = jnp.bfloat16
NN = (((1,), (0,)), ((), ()))
NT = (((1,), (1,)), ((), ()))
TN = (((0,), (0,)), ((), ()))


def mm(a, b, dims=NN):
    return lax.dot_general(a, b, dims, preferred_element_type=F32)


def wait_for(ref, sem):
    pltpu.make_async_copy(ref, ref, sem).wait()


def pack(rows, parts, half):
    m = rows.shape[0] // parts
    return [
        jnp.concatenate(
            [rows[p * m:(p + 1) * m, :half], rows[p * m:(p + 1) * m, half:]], axis=0
        ).astype(BF16)
        for p in range(parts)
    ]


def unpack(blocks, parts):
    m = blocks.shape[1] // 2
    wide = [blocks[p].astype(F32) for p in range(parts)]
    left = jnp.concatenate([b[:m] for b in wide], axis=0)
    right = jnp.concatenate([b[m:] for b in wide], axis=0)
    return jnp.concatenate([left, right], axis=1).astype(BF16)


def kernel(
    side, chunks,
    tok_hbm, cot_hbm, w_row, route_row, swap, wu_hbm, wd_hbm,
    mixed, token_grads, combine_grads, dwu, dwd,
    tok, cot, wu, wd,
    send_a, send_b, recv_a, recv_b, xg, wu_far, wd_far, acc, hid, pg,
    out_send, out_recv, dwu_send, dwd_send, dwu_recv, dwd_recv,
    pick, pick_t, w_col, cg, source,
    a_out, a_in, b_out, b_in, y_out, y_in, f_out, f_in, o_out, o_in, d_out, d_in, load, load_w,
):
    nt, width = tok.shape
    slots = side * side * CAP
    half = CHUNK // 2
    expert, y = lax.axis_index("expert"), lax.axis_index("replica")
    z, k = expert // side, expert % side
    core = k % 2
    odd = 1 - (y + core) % 2 * 2
    row_pal = (expert, (y + odd + 4) % 4)
    block_pal = (expert, (y - odd + 4) % 4)
    steps = 2 * chunks

    barrier = pltpu.get_barrier_semaphore()
    for d in range(1, side):
        pl.semaphore_signal(barrier, inc=1, device_id=((z + d) % side * side + k, y), device_id_type=MESH)
        pl.semaphore_signal(barrier, inc=1, device_id=(z * side + (k + d) % side, y), device_id_type=MESH)
    pl.semaphore_signal(barrier, inc=1, device_id=row_pal, device_id_type=MESH)
    pl.semaphore_signal(barrier, inc=1, device_id=block_pal, device_id_type=MESH)

    def columns(j):
        return pl.ds(pl.multiple_of(j * CHUNK, CHUNK), CHUNK)

    def tok_load(j):
        return pltpu.make_async_copy(tok_hbm.at[:, columns(j)], tok.at[:, columns(j)], load.at[j])

    def cot_load(j):
        return pltpu.make_async_copy(cot_hbm.at[:, columns(j)], cot.at[:, columns(j)], load.at[chunks + j])

    wu_load = pltpu.make_async_copy(wu_hbm, wu, load_w.at[0])
    wd_load = pltpu.make_async_copy(wd_hbm, wd, load_w.at[1])
    for j in range(chunks):
        tok_load(j).start()
    wu_load.start()
    for j in range(chunks):
        cot_load(j).start()
    wd_load.start()

    def far_weight(i, go):
        j = i % chunks

        @pl.when(i < chunks)
        def _():
            copy = pltpu.make_async_remote_copy(
                wu_hbm.at[columns(j), :], wu_far.at[j], f_out.at[i], f_in.at[i],
                device_id=block_pal, device_id_type=MESH)
            go(copy)

        @pl.when(i >= chunks)
        def _():
            copy = pltpu.make_async_remote_copy(
                wd_hbm.at[:, columns(j)], wd_far.at[j], f_out.at[i], f_in.at[i],
                device_id=block_pal, device_id_type=MESH)
            go(copy)

    pl.semaphore_wait(barrier, 2 * side)
    for i in range(AHEAD):
        far_weight(jnp.int32(i), lambda copy: copy.start())

    down = lax.broadcasted_iota(jnp.int32, (nt, nt), 0)
    across = lax.broadcasted_iota(jnp.int32, (nt, nt), 1)
    eye = down == across
    routes = jnp.broadcast_to(route_row[...].astype(F32), (nt, nt))
    route_col = jnp.sum(jnp.where(eye, routes, 0.0), axis=1, keepdims=True)
    w_col[...] = jnp.sum(jnp.where(eye, jnp.broadcast_to(w_row[...], (nt, nt)), 0.0), axis=1, keepdims=True)
    same = routes == route_col
    rank_row = jnp.sum(jnp.where(same & (down < across), 1.0, 0.0), axis=0, keepdims=True)
    rank_col = jnp.sum(jnp.where(same & (across < down), 1.0, 0.0), axis=1, keepdims=True)
    limit = float(side * side)
    slot_row = jnp.where(routes[:1] < limit, routes[:1] * CAP + rank_row, float(slots))
    slot_col = jnp.where(route_col < limit, route_col * CAP + rank_col, float(slots))
    at_slot = lax.broadcasted_iota(jnp.int32, (slots, nt), 0).astype(F32)
    pick[...] = jnp.where(at_slot == slot_row, 1.0, 0.0).astype(BF16)
    at_slot = lax.broadcasted_iota(jnp.int32, (nt, slots), 1).astype(F32)
    pick_t[...] = jnp.where(at_slot == slot_col, 1.0, 0.0).astype(BF16)
    acc[...] = jnp.zeros_like(acc)
    cg[...] = jnp.zeros_like(cg)

    order = sorted(range(1, side), key=lambda d: -min(d, side - d))

    def exchange_a(i, j):
        for d in order:
            to = (z + d) % side
            pltpu.make_async_remote_copy(
                send_a.at[j, to], recv_a.at[i, z], a_out.at[j], a_in.at[i],
                device_id=(to * side + k, y), device_id_type=MESH,
            ).start()
        pltpu.make_async_copy(send_a.at[j, z], recv_a.at[i, z], a_in.at[i]).start()

    def exchange_b(i, j):
        for d in order:
            to = (k + d) % side
            pltpu.make_async_remote_copy(
                send_b.at[j, to], recv_b.at[i, k], b_out.at[j], b_in.at[i],
                device_id=(z * side + to, y), device_id_type=MESH,
            ).start()
        pltpu.make_async_copy(send_b.at[j, k], recv_b.at[i, k], b_in.at[i]).start()

    def sent_a(j):
        wait_for(send_a.at[j, pl.ds(0, side - 1)], a_out.at[j])

    def sent_b(j):
        wait_for(send_b.at[j, pl.ds(0, side - 1)], b_out.at[j])

    def swapped(ref, i):
        blocks = ref[i]
        flat = blocks.reshape(blocks.shape[0] * blocks.shape[1], half)
        return mm(swap[...], flat).astype(BF16).reshape(blocks.shape)

    def step_a(i):
        j = i % chunks

        @pl.when(i < chunks)
        def _():
            tok_load(j).wait()
            source[...] = tok[:, columns(j)]

        @pl.when(i >= chunks)
        def _():
            sent_a(j)
            cot_load(j).wait()
            source[...] = (w_col[...] * cot[:, columns(j)].astype(F32)).astype(BF16)

        for p, block in enumerate(pack(mm(pick[...], source[...]), side, half)):
            send_a[j, p] = block
        exchange_a(i, j)

    def step_b(i):
        j = i % chunks
        wait_for(recv_a.at[i], a_in.at[i])

        @pl.when(i >= chunks)
        def _():
            sent_b(j)

        send_b[j] = swapped(recv_a, i)
        exchange_b(i, j)

    def row_copy(i):
        return pltpu.make_async_remote_copy(
            xg.at[i, pl.ds(0, slots)], xg.at[i, pl.ds(slots, slots)], y_out.at[i], y_in.at[i],
            device_id=row_pal, device_id_type=MESH)

    def step_c(i):
        wait_for(recv_b.at[i], b_in.at[i])
        xg[i, pl.ds(0, slots)] = unpack(recv_b[i], side)
        row_copy(i).start()

    def step_d(i):
        j = i % chunks
        row_copy(i).wait_recv()
        far_weight(i, lambda copy: copy.wait_recv())

        @pl.when(i == 0)
        def _():
            wu_load.wait()

        @pl.when(i == chunks)
        def _():
            wd_load.wait()

        @pl.when(i < chunks)
        def _():
            acc[0] += mm(xg[i], wu[columns(j), :])
            acc[1] += mm(xg[i], wu_far[j])

        @pl.when(i >= chunks)
        def _():
            acc[2] += mm(xg[i], wd[:, columns(j)], NT)
            acc[3] += mm(xg[i], wd_far[j], NT)

    def at(i, lag, step):
        @pl.when((i >= lag) & (i < steps + lag))
        def _():
            step(i - lag)

    def sigmoid(v):
        return 1.0 / (1.0 + jnp.exp(-v))

    def forward():
        for b in range(2):
            pre = acc[b]
            hid[b] = (pre * sigmoid(pre)).astype(BF16)

    def backward():
        for b in range(2):
            pre = acc[b]
            s = sigmoid(pre)
            pg[b] = (acc[2 + b] * (s * (1.0 + pre * (1.0 - s)))).astype(BF16)

    def out_copy(i):
        j = i % chunks
        return pltpu.make_async_remote_copy(
            out_send.at[j], out_recv.at[i], o_out.at[j], o_in.at[i],
            device_id=row_pal, device_id_type=MESH)

    def dwd_copy(i):
        j = i % chunks
        return pltpu.make_async_remote_copy(
            dwd_send.at[j], dwd_recv.at[j], d_out.at[i], d_in.at[i],
            device_id=block_pal, device_id_type=MESH)

    def dwu_copy(i):
        j = i % chunks
        return pltpu.make_async_remote_copy(
            dwu_send.at[j], dwu_recv.at[j], d_out.at[i], d_in.at[i],
            device_id=block_pal, device_id_type=MESH)

    def out_rows(j, rows):
        return mm(hid[0, rows], wd[:, columns(j)]) + mm(hid[1, rows], wd_far[j])

    def grad_rows(j, rows):
        return mm(pg[0, rows], wu[columns(j), :], NT) + mm(pg[1, rows], wu_far[j], NT)

    near, far = pl.ds(0, slots), pl.ds(slots, slots)

    def step_e(i):
        j = i % chunks

        @pl.when(i < chunks)
        def _():
            out_send[j] = out_rows(j, far).astype(BF16)
            out_copy(i).start()

        @pl.when(i >= chunks)
        def _():
            out_copy(i).wait_send()
            out_send[j] = grad_rows(j, far).astype(BF16)
            out_copy(i).start()

    def step_w(i):
        j = i % chunks

        @pl.when(i < chunks)
        def _():
            dwd_send[j] = mm(hid[1], xg[chunks + j], TN).astype(BF16)
            dwd_copy(i).start()

        @pl.when(i >= chunks)
        def _():
            dwu_send[j] = mm(xg[j], pg[1], TN).astype(BF16)
            dwu_copy(i).start()

    def step_f(i):
        j = i % chunks
        out_copy(i).wait_recv()
        sent_b(j)

        @pl.when(i < chunks)
        def _():
            for p, block in enumerate(pack(out_rows(j, near) + out_recv[i].astype(F32), side, half)):
                send_b[j, p] = block

        @pl.when(i >= chunks)
        def _():
            for p, block in enumerate(pack(grad_rows(j, near) + out_recv[i].astype(F32), side, half)):
                send_b[j, p] = block

        exchange_b(steps + i, j)

    def step_g(i):
        j = i % chunks
        wait_for(recv_b.at[steps + i], b_in.at[steps + i])
        sent_a(j)
        send_a[j] = swapped(recv_b, steps + i)
        exchange_a(steps + i, j)

    def step_h(i):
        j = i % chunks
        wait_for(recv_a.at[steps + i], a_in.at[steps + i])
        rows = mm(pick_t[...], unpack(recv_a[steps + i], side))
        scaled = (w_col[...] * rows).astype(BF16)

        @pl.when(i < chunks)
        def _():
            mixed[:, columns(j)] = scaled
            cg[...] += jnp.sum(rows * cot[:, columns(j)].astype(F32), axis=1, keepdims=True)

        @pl.when(i >= chunks)
        def _():
            token_grads[:, columns(j)] = scaled

    def step_i(i):
        j = i % chunks

        @pl.when(i < chunks)
        def _():
            dwd_copy(i).wait_recv()
            dwd[:, columns(j)] = (mm(hid[0], xg[chunks + j], TN) + dwd_recv[j].astype(F32)).astype(BF16)

        @pl.when(i >= chunks)
        def _():
            dwu_copy(i).wait_recv()
            dwu[columns(j), :] = (mm(xg[j], pg[0], TN) + dwu_recv[j].astype(F32)).astype(BF16)

    begin = chunks + LAG_D

    def turn(n, _):
        at(n, 0, step_a)

        @pl.when(n + AHEAD < steps)
        def _():
            far_weight(n + AHEAD, lambda copy: copy.start())

        at(n, LAG_B, step_b)
        at(n, LAG_C, step_c)
        at(n, LAG_D, step_d)
        pl.when(n == begin - 1)(forward)
        pl.when(n == begin + chunks - 1)(backward)
        at(n, begin, step_e)
        at(n, begin + LAG_F, step_f)
        at(n, begin + LAG_W, step_w)
        at(n, begin + LAG_G, step_g)
        at(n, begin + LAG_H, step_h)
        at(n, begin + LAG_I, step_i)
        return 0

    lax.fori_loop(0, begin + steps + max(LAG_H, LAG_I), turn, 0)

    combine_grads[...] = jnp.sum(jnp.where(eye, jnp.broadcast_to(cg[...], (nt, nt)), 0.0), axis=0, keepdims=True)

    def drain(j, _):
        sent_a(j)
        sent_b(j)
        out_copy(j + chunks).wait_send()
        dwd_copy(j).wait_send()
        dwu_copy(j + chunks).wait_send()
        return 0

    lax.fori_loop(0, chunks, drain, 0)

    def drain_all(i, _):
        row_copy(i).wait_send()
        far_weight(i, lambda copy: copy.wait_send())
        return 0

    lax.fori_loop(0, steps, drain_all, 0)


PIECES = 4


def hand_over(*refs):
    given, result, stores = refs[:4], refs[5:9], refs[10]
    copies = []
    for a in range(4):
        rows = given[a].shape[0] // PIECES
        for p in range(PIECES):
            at = pl.ds(p * rows, rows)
            copies.append(pltpu.make_async_copy(given[a].at[at], result[a].at[at], stores.at[a * PIECES + p]))
    for copy in copies:
        copy.start()
    refs[9][...] = refs[4][...].reshape(refs[9].shape)
    for copy in copies:
        copy.wait()


def swap_matrix(side):
    n = side * 2 * side * CAP
    index = np.arange(n).reshape(side, 2, side, CAP)
    source = index.transpose(2, 1, 0, 3).reshape(-1)
    matrix = np.zeros((n, n), np.float32)
    matrix[np.arange(n), source] = 1.0
    return matrix.astype(jnp.bfloat16)


def body(side, tokens, routes, combine_weights, up_weight, down_weight, cotangent):
    nt, width = tokens.shape
    block = up_weight.shape[2]
    chunks = width // CHUNK
    slots = side * side * CAP
    half = CHUNK // 2
    steps = 2 * chunks
    vmem = pl.BlockSpec(memory_space=pltpu.VMEM)
    hbm = pl.BlockSpec(memory_space=pl.ANY)
    message = (side, 2 * side * CAP, half)
    dma = pltpu.SemaphoreType.DMA
    mixed, token_grads, combine_grads, up_grads, down_grads = pl.pallas_call(
        functools.partial(kernel, side, chunks),
        out_shape=(
            pltpu.VMEM((nt, width), BF16),
            pltpu.VMEM((nt, width), BF16),
            pltpu.VMEM((1, nt), F32),
            pltpu.VMEM((width, block), BF16),
            pltpu.VMEM((block, width), BF16),
        ),
        in_specs=[hbm, hbm, vmem, vmem, vmem, hbm, hbm],
        out_specs=(vmem,) * 5,
        scratch_shapes=[
            pltpu.VMEM((nt, width), BF16),
            pltpu.VMEM((nt, width), BF16),
            pltpu.VMEM((width, block), BF16),
            pltpu.VMEM((block, width), BF16),
            pltpu.VMEM((chunks,) + message, BF16),
            pltpu.VMEM((chunks,) + message, BF16),
            pltpu.VMEM((2 * steps,) + message, BF16),
            pltpu.VMEM((2 * steps,) + message, BF16),
            pltpu.VMEM((steps, 2 * slots, CHUNK), BF16),
            pltpu.VMEM((chunks, CHUNK, block), BF16),
            pltpu.VMEM((chunks, block, CHUNK), BF16),
            pltpu.VMEM((4, 2 * slots, block), F32),
            pltpu.VMEM((2, 2 * slots, block), BF16),
            pltpu.VMEM((2, 2 * slots, block), BF16),
            pltpu.VMEM((chunks, slots, CHUNK), BF16),
            pltpu.VMEM((steps, slots, CHUNK), BF16),
            pltpu.VMEM((chunks, CHUNK, block), BF16),
            pltpu.VMEM((chunks, block, CHUNK), BF16),
            pltpu.VMEM((chunks, CHUNK, block), BF16),
            pltpu.VMEM((chunks, block, CHUNK), BF16),
            pltpu.VMEM((slots, nt), BF16),
            pltpu.VMEM((nt, slots), BF16),
            pltpu.VMEM((nt, 1), F32),
            pltpu.VMEM((nt, 1), F32),
            pltpu.VMEM((nt, CHUNK), BF16),
            dma((chunks,)), dma((2 * steps,)),
            dma((chunks,)), dma((2 * steps,)),
            dma((steps,)), dma((steps,)),
            dma((steps,)), dma((steps,)),
            dma((chunks,)), dma((steps,)),
            dma((steps,)), dma((steps,)),
            dma((steps,)), dma((2,)),
        ],
        compiler_params=pltpu.CompilerParams(
            collective_id=0, has_side_effects=True, vmem_limit_bytes=50 * 1024 * 1024
        ),
    )(
        tokens, cotangent, combine_weights[None], routes[None],
        jnp.asarray(swap_matrix(side)), up_weight[0], down_weight[0],
    )
    large = (mixed, token_grads, up_grads, down_grads)
    mixed, token_grads, up_grads, down_grads, combine_grads = pl.pallas_call(
        hand_over,
        out_shape=[jax.ShapeDtypeStruct(a.shape, a.dtype) for a in large] + [jax.ShapeDtypeStruct((nt,), F32)],
        in_specs=[vmem] * 5,
        out_specs=[hbm] * 4 + [vmem],
        scratch_shapes=[dma((4 * PIECES,))],
        compiler_params=pltpu.CompilerParams(vmem_limit_bytes=4 * 1024 * 1024),
    )(*large, combine_grads)
    return mixed, token_grads, combine_grads, up_grads[None], down_grads[None]


def solution(mesh):
    side = math.isqrt(mesh.shape["expert"])
    row, vector = P(("expert", "replica"), None), P(("expert", "replica"))
    up, down = P("expert", None, "replica"), P("expert", "replica", None)
    return jax.shard_map(
        functools.partial(body, side),
        mesh=mesh,
        in_specs=(row, vector, vector, up, down, row),
        out_specs=(row, row, vector, up, down),
        check_vma=False,
    )
```

```python
import functools
import math

import jax
import jax.numpy as jnp
import numpy as np
from jax import lax
from jax.experimental import pallas as pl
from jax.experimental.pallas import tpu as pltpu
from jax.sharding import PartitionSpec as P

CAP = 3
CHUNK = 512
LAG_B, LAG_C, LAG_D = 1, 2, 4
LAG_F, LAG_G, LAG_H, LAG_W, LAG_I = 2, 3, 5, 4, 8
AHEAD = 6
MESH = pl.DeviceIdType.MESH
F32 = jnp.float32
BF16 = jnp.bfloat16
NN = (((1,), (0,)), ((), ()))
NT = (((1,), (1,)), ((), ()))
TN = (((0,), (0,)), ((), ()))


def mm(a, b, dims=NN):
    return lax.dot_general(a, b, dims, preferred_element_type=F32)


def wait_for(ref, sem):
    pltpu.make_async_copy(ref, ref, sem).wait()


def pack(rows, parts, half):
    m = rows.shape[0] // parts
    return [
        jnp.concatenate(
            [rows[p * m:(p + 1) * m, :half], rows[p * m:(p + 1) * m, half:]], axis=0
        ).astype(BF16)
        for p in range(parts)
    ]


def unpack(blocks, parts):
    m = blocks.shape[1] // 2
    wide = [blocks[p].astype(F32) for p in range(parts)]
    left = jnp.concatenate([b[:m] for b in wide], axis=0)
    right = jnp.concatenate([b[m:] for b in wide], axis=0)
    return jnp.concatenate([left, right], axis=1).astype(BF16)


def kernel(
    side, chunks,
    tok_hbm, cot_hbm, w_hbm, route_hbm, swap_hbm, wu_hbm, wd_hbm,
    mixed, token_grads, combine_grads, dwu, dwd,
    tok, cot, wu, wd, w_row, route_row, swap,
    send_a, send_b, recv_a, recv_b, xg, wu_far, wd_far, acc, hid, pg,
    out_send, out_recv, dwu_send, dwd_send, dwu_recv, dwd_recv,
    pick, pick_t, w_col, cg, source,
    a_out, a_in, b_out, b_in, y_out, y_in, f_out, f_in, o_out, o_in, d_out, d_in, load, load_w,
):
    nt, width = tok.shape
    slots = side * side * CAP
    half = CHUNK // 2
    expert, y = lax.axis_index("expert"), lax.axis_index("replica")
    z, k = expert // side, expert % side
    core = k % 2
    odd = 1 - (y + core) % 2 * 2
    row_pal = (expert, (y + odd + 4) % 4)
    block_pal = (expert, (y - odd + 4) % 4)
    steps = 2 * chunks

    barrier = pltpu.get_barrier_semaphore()
    for d in range(1, side):
        pl.semaphore_signal(barrier, inc=1, device_id=((z + d) % side * side + k, y), device_id_type=MESH)
        pl.semaphore_signal(barrier, inc=1, device_id=(z * side + (k + d) % side, y), device_id_type=MESH)
    pl.semaphore_signal(barrier, inc=1, device_id=row_pal, device_id_type=MESH)
    pl.semaphore_signal(barrier, inc=1, device_id=block_pal, device_id_type=MESH)

    def columns(j):
        return pl.ds(pl.multiple_of(j * CHUNK, CHUNK), CHUNK)

    def tok_load(j):
        return pltpu.make_async_copy(tok_hbm.at[:, columns(j)], tok.at[:, columns(j)], load.at[j])

    def cot_load(j):
        return pltpu.make_async_copy(cot_hbm.at[:, columns(j)], cot.at[:, columns(j)], load.at[chunks + j])

    wu_load = pltpu.make_async_copy(wu_hbm, wu, load_w.at[0])
    wd_load = pltpu.make_async_copy(wd_hbm, wd, load_w.at[1])
    small = [
        pltpu.make_async_copy(a, b, load_w.at[2 + i])
        for i, (a, b) in enumerate(((w_hbm, w_row), (route_hbm, route_row), (swap_hbm, swap)))
    ]
    for copy in small:
        copy.start()
    for j in range(chunks):
        tok_load(j).start()
    wu_load.start()
    for j in range(chunks):
        cot_load(j).start()
    wd_load.start()

    def far_weight(i, go):
        j = i % chunks

        @pl.when(i < chunks)
        def _():
            copy = pltpu.make_async_remote_copy(
                wu_hbm.at[columns(j), :], wu_far.at[j], f_out.at[i], f_in.at[i],
                device_id=block_pal, device_id_type=MESH)
            go(copy)

        @pl.when(i >= chunks)
        def _():
            copy = pltpu.make_async_remote_copy(
                wd_hbm.at[:, columns(j)], wd_far.at[j], f_out.at[i], f_in.at[i],
                device_id=block_pal, device_id_type=MESH)
            go(copy)

    pl.semaphore_wait(barrier, 2 * side)
    for i in range(AHEAD):
        far_weight(jnp.int32(i), lambda copy: copy.start())

    for copy in small:
        copy.wait()

    down = lax.broadcasted_iota(jnp.int32, (nt, nt), 0)
    across = lax.broadcasted_iota(jnp.int32, (nt, nt), 1)
    eye = down == across
    routes = jnp.broadcast_to(route_row[...].astype(F32), (nt, nt))
    route_col = jnp.sum(jnp.where(eye, routes, 0.0), axis=1, keepdims=True)
    w_col[...] = jnp.sum(jnp.where(eye, jnp.broadcast_to(w_row[...], (nt, nt)), 0.0), axis=1, keepdims=True)
    same = routes == route_col
    rank_row = jnp.sum(jnp.where(same & (down < across), 1.0, 0.0), axis=0, keepdims=True)
    rank_col = jnp.sum(jnp.where(same & (across < down), 1.0, 0.0), axis=1, keepdims=True)
    limit = float(side * side)
    slot_row = jnp.where(routes[:1] < limit, routes[:1] * CAP + rank_row, float(slots))
    slot_col = jnp.where(route_col < limit, route_col * CAP + rank_col, float(slots))
    at_slot = lax.broadcasted_iota(jnp.int32, (slots, nt), 0).astype(F32)
    pick[...] = jnp.where(at_slot == slot_row, 1.0, 0.0).astype(BF16)
    at_slot = lax.broadcasted_iota(jnp.int32, (nt, slots), 1).astype(F32)
    pick_t[...] = jnp.where(at_slot == slot_col, 1.0, 0.0).astype(BF16)
    acc[...] = jnp.zeros_like(acc)
    cg[...] = jnp.zeros_like(cg)

    order = sorted(range(1, side), key=lambda d: -min(d, side - d))

    def exchange_a(i, j):
        for d in order:
            to = (z + d) % side
            pltpu.make_async_remote_copy(
                send_a.at[j, to], recv_a.at[i, z], a_out.at[j], a_in.at[i],
                device_id=(to * side + k, y), device_id_type=MESH,
            ).start()
        pltpu.make_async_copy(send_a.at[j, z], recv_a.at[i, z], a_in.at[i]).start()

    def exchange_b(i, j):
        for d in order:
            to = (k + d) % side
            pltpu.make_async_remote_copy(
                send_b.at[j, to], recv_b.at[i, k], b_out.at[j], b_in.at[i],
                device_id=(z * side + to, y), device_id_type=MESH,
            ).start()
        pltpu.make_async_copy(send_b.at[j, k], recv_b.at[i, k], b_in.at[i]).start()

    def sent_a(j):
        wait_for(send_a.at[j, pl.ds(0, side - 1)], a_out.at[j])

    def sent_b(j):
        wait_for(send_b.at[j, pl.ds(0, side - 1)], b_out.at[j])

    def swapped(ref, i):
        blocks = ref[i]
        flat = blocks.reshape(blocks.shape[0] * blocks.shape[1], half)
        return mm(swap[...], flat).astype(BF16).reshape(blocks.shape)

    def step_a(i):
        j = i % chunks

        @pl.when(i < chunks)
        def _():
            tok_load(j).wait()
            source[...] = tok[:, columns(j)]

        @pl.when(i >= chunks)
        def _():
            sent_a(j)
            cot_load(j).wait()
            source[...] = (w_col[...] * cot[:, columns(j)].astype(F32)).astype(BF16)

        for p, block in enumerate(pack(mm(pick[...], source[...]), side, half)):
            send_a[j, p] = block
        exchange_a(i, j)

    def step_b(i):
        j = i % chunks
        wait_for(recv_a.at[i], a_in.at[i])

        @pl.when(i >= chunks)
        def _():
            sent_b(j)

        send_b[j] = swapped(recv_a, i)
        exchange_b(i, j)

    def row_copy(i):
        return pltpu.make_async_remote_copy(
            xg.at[i, pl.ds(0, slots)], xg.at[i, pl.ds(slots, slots)], y_out.at[i], y_in.at[i],
            device_id=row_pal, device_id_type=MESH)

    def step_c(i):
        wait_for(recv_b.at[i], b_in.at[i])
        xg[i, pl.ds(0, slots)] = unpack(recv_b[i], side)
        row_copy(i).start()

    def step_d(i):
        j = i % chunks
        row_copy(i).wait()
        far_weight(i, lambda copy: copy.wait())

        @pl.when(i == 0)
        def _():
            wu_load.wait()

        @pl.when(i == chunks)
        def _():
            wd_load.wait()

        @pl.when(i < chunks)
        def _():
            acc[0] += mm(xg[i], wu[columns(j), :])
            acc[1] += mm(xg[i], wu_far[j])

        @pl.when(i >= chunks)
        def _():
            acc[2] += mm(xg[i], wd[:, columns(j)], NT)
            acc[3] += mm(xg[i], wd_far[j], NT)

    def at(i, lag, step):
        @pl.when((i >= lag) & (i < steps + lag))
        def _():
            step(i - lag)

    def sigmoid(v):
        return 1.0 / (1.0 + jnp.exp(-v))

    def forward():
        for b in range(2):
            pre = acc[b]
            hid[b] = (pre * sigmoid(pre)).astype(BF16)

    def backward():
        for b in range(2):
            pre = acc[b]
            s = sigmoid(pre)
            pg[b] = (acc[2 + b] * (s * (1.0 + pre * (1.0 - s)))).astype(BF16)

    def out_copy(i):
        j = i % chunks
        return pltpu.make_async_remote_copy(
            out_send.at[j], out_recv.at[i], o_out.at[j], o_in.at[i],
            device_id=row_pal, device_id_type=MESH)

    def dwd_copy(i):
        j = i % chunks
        return pltpu.make_async_remote_copy(
            dwd_send.at[j], dwd_recv.at[j], d_out.at[i], d_in.at[i],
            device_id=block_pal, device_id_type=MESH)

    def dwu_copy(i):
        j = i % chunks
        return pltpu.make_async_remote_copy(
            dwu_send.at[j], dwu_recv.at[j], d_out.at[i], d_in.at[i],
            device_id=block_pal, device_id_type=MESH)

    def out_rows(j, rows):
        return mm(hid[0, rows], wd[:, columns(j)]) + mm(hid[1, rows], wd_far[j])

    def grad_rows(j, rows):
        return mm(pg[0, rows], wu[columns(j), :], NT) + mm(pg[1, rows], wu_far[j], NT)

    near, far = pl.ds(0, slots), pl.ds(slots, slots)

    def step_e(i):
        j = i % chunks

        @pl.when(i < chunks)
        def _():
            out_send[j] = out_rows(j, far).astype(BF16)
            out_copy(i).start()

        @pl.when(i >= chunks)
        def _():
            out_send[j] = grad_rows(j, far).astype(BF16)
            out_copy(i).start()

    def step_w(i):
        j = i % chunks

        @pl.when(i < chunks)
        def _():
            dwd_send[j] = mm(hid[1], xg[chunks + j], TN).astype(BF16)
            dwd_copy(i).start()

        @pl.when(i >= chunks)
        def _():
            dwu_send[j] = mm(xg[j], pg[1], TN).astype(BF16)
            dwu_copy(i).start()

    def step_f(i):
        j = i % chunks
        out_copy(i).wait()
        sent_b(j)

        @pl.when(i < chunks)
        def _():
            for p, block in enumerate(pack(out_rows(j, near) + out_recv[i].astype(F32), side, half)):
                send_b[j, p] = block

        @pl.when(i >= chunks)
        def _():
            for p, block in enumerate(pack(grad_rows(j, near) + out_recv[i].astype(F32), side, half)):
                send_b[j, p] = block

        exchange_b(steps + i, j)

    def step_g(i):
        j = i % chunks
        wait_for(recv_b.at[steps + i], b_in.at[steps + i])
        sent_a(j)
        send_a[j] = swapped(recv_b, steps + i)
        exchange_a(steps + i, j)

    def step_h(i):
        j = i % chunks
        wait_for(recv_a.at[steps + i], a_in.at[steps + i])
        rows = mm(pick_t[...], unpack(recv_a[steps + i], side))
        scaled = (w_col[...] * rows).astype(BF16)

        @pl.when(i < chunks)
        def _():
            mixed[:, columns(j)] = scaled
            cg[...] += jnp.sum(rows * cot[:, columns(j)].astype(F32), axis=1, keepdims=True)

        @pl.when(i >= chunks)
        def _():
            token_grads[:, columns(j)] = scaled
            sent_a(j)
            sent_b(j)

    def step_i(i):
        j = i % chunks

        @pl.when(i < chunks)
        def _():
            dwd_copy(i).wait()
            dwd[:, columns(j)] = (mm(hid[0], xg[chunks + j], TN) + dwd_recv[j].astype(F32)).astype(BF16)

        @pl.when(i >= chunks)
        def _():
            dwu_copy(i).wait()
            dwu[columns(j), :] = (mm(xg[j], pg[0], TN) + dwu_recv[j].astype(F32)).astype(BF16)

    begin = chunks + LAG_D

    def finish_combine_grads():
        combine_grads[...] = jnp.sum(
            jnp.where(eye, jnp.broadcast_to(cg[...], (nt, nt)), 0.0), axis=0, keepdims=True)

    def turn(n, _):
        at(n, 0, step_a)

        @pl.when(n + AHEAD < steps)
        def _():
            far_weight(n + AHEAD, lambda copy: copy.start())

        at(n, LAG_B, step_b)
        at(n, LAG_C, step_c)
        at(n, LAG_D, step_d)
        pl.when(n == begin - 1)(forward)
        pl.when(n == begin + chunks - 1)(backward)
        at(n, begin, step_e)
        at(n, begin + LAG_F, step_f)
        at(n, begin + LAG_W, step_w)
        at(n, begin + LAG_G, step_g)
        at(n, begin + LAG_H, step_h)
        pl.when(n == begin + chunks + LAG_H)(finish_combine_grads)
        at(n, begin + LAG_I, step_i)
        return 0

    lax.fori_loop(0, begin + steps + max(LAG_H, LAG_I), turn, 0)


PIECES = 4


def hand_over(*refs):
    given, result, stores = refs[:4], refs[5:9], refs[10]
    copies = []
    for a in range(4):
        rows = given[a].shape[0] // PIECES
        for p in range(PIECES):
            at = pl.ds(p * rows, rows)
            copies.append(pltpu.make_async_copy(given[a].at[at], result[a].at[at], stores.at[a * PIECES + p]))
    for copy in copies:
        copy.start()
    refs[9][...] = refs[4][...].reshape(refs[9].shape)
    for copy in copies:
        copy.wait()


def swap_matrix(side):
    n = side * 2 * side * CAP
    index = np.arange(n).reshape(side, 2, side, CAP)
    source = index.transpose(2, 1, 0, 3).reshape(-1)
    matrix = np.zeros((n, n), np.float32)
    matrix[np.arange(n), source] = 1.0
    return matrix.astype(jnp.bfloat16)


def body(side, tokens, routes, combine_weights, up_weight, down_weight, cotangent):
    nt, width = tokens.shape
    block = up_weight.shape[2]
    chunks = width // CHUNK
    slots = side * side * CAP
    half = CHUNK // 2
    steps = 2 * chunks
    vmem = pl.BlockSpec(memory_space=pltpu.VMEM)
    hbm = pl.BlockSpec(memory_space=pl.ANY)
    message = (side, 2 * side * CAP, half)
    dma = pltpu.SemaphoreType.DMA
    mixed, token_grads, combine_grads, up_grads, down_grads = pl.pallas_call(
        functools.partial(kernel, side, chunks),
        out_shape=(
            pltpu.VMEM((nt, width), BF16),
            pltpu.VMEM((nt, width), BF16),
            pltpu.VMEM((1, nt), F32),
            pltpu.VMEM((width, block), BF16),
            pltpu.VMEM((block, width), BF16),
        ),
        in_specs=[hbm] * 7,
        out_specs=(vmem,) * 5,
        scratch_shapes=[
            pltpu.VMEM((nt, width), BF16),
            pltpu.VMEM((nt, width), BF16),
            pltpu.VMEM((width, block), BF16),
            pltpu.VMEM((block, width), BF16),
            pltpu.VMEM((1, nt), F32),
            pltpu.VMEM((1, nt), jnp.int32),
            pltpu.VMEM((2 * slots, 2 * slots), BF16),
            pltpu.VMEM((chunks,) + message, BF16),
            pltpu.VMEM((chunks,) + message, BF16),
            pltpu.VMEM((2 * steps,) + message, BF16),
            pltpu.VMEM((2 * steps,) + message, BF16),
            pltpu.VMEM((steps, 2 * slots, CHUNK), BF16),
            pltpu.VMEM((chunks, CHUNK, block), BF16),
            pltpu.VMEM((chunks, block, CHUNK), BF16),
            pltpu.VMEM((4, 2 * slots, block), F32),
            pltpu.VMEM((2, 2 * slots, block), BF16),
            pltpu.VMEM((2, 2 * slots, block), BF16),
            pltpu.VMEM((chunks, slots, CHUNK), BF16),
            pltpu.VMEM((steps, slots, CHUNK), BF16),
            pltpu.VMEM((chunks, CHUNK, block), BF16),
            pltpu.VMEM((chunks, block, CHUNK), BF16),
            pltpu.VMEM((chunks, CHUNK, block), BF16),
            pltpu.VMEM((chunks, block, CHUNK), BF16),
            pltpu.VMEM((slots, nt), BF16),
            pltpu.VMEM((nt, slots), BF16),
            pltpu.VMEM((nt, 1), F32),
            pltpu.VMEM((nt, 1), F32),
            pltpu.VMEM((nt, CHUNK), BF16),
            dma((chunks,)), dma((2 * steps,)),
            dma((chunks,)), dma((2 * steps,)),
            dma((steps,)), dma((steps,)),
            dma((steps,)), dma((steps,)),
            dma((chunks,)), dma((steps,)),
            dma((steps,)), dma((steps,)),
            dma((steps,)), dma((5,)),
        ],
        compiler_params=pltpu.CompilerParams(
            collective_id=0, has_side_effects=True, vmem_limit_bytes=50 * 1024 * 1024
        ),
    )(
        tokens, cotangent, combine_weights[None], routes[None],
        jnp.asarray(swap_matrix(side)), up_weight[0], down_weight[0],
    )
    large = (mixed, token_grads, up_grads, down_grads)
    mixed, token_grads, up_grads, down_grads, combine_grads = pl.pallas_call(
        hand_over,
        out_shape=[jax.ShapeDtypeStruct(a.shape, a.dtype) for a in large] + [jax.ShapeDtypeStruct((nt,), F32)],
        in_specs=[vmem] * 5,
        out_specs=[hbm] * 4 + [vmem],
        scratch_shapes=[dma((4 * PIECES,))],
        compiler_params=pltpu.CompilerParams(vmem_limit_bytes=4 * 1024 * 1024),
    )(*large, combine_grads)
    return mixed, token_grads, combine_grads, up_grads[None], down_grads[None]


def solution(mesh):
    side = math.isqrt(mesh.shape["expert"])
    row, vector = P(("expert", "replica"), None), P(("expert", "replica"))
    up, down = P("expert", None, "replica"), P("expert", "replica", None)
    return jax.shard_map(
        functools.partial(body, side),
        mesh=mesh,
        in_specs=(row, vector, vector, up, down, row),
        out_specs=(row, row, vector, up, down),
        check_vma=False,
    )
```
